256 devices in a mesh: frame: 32 (over z_lo, x, core), head: 8 (over z_hi, y).
Axes of the slice: x: 4, y: 4, z: 8 (z_hi: 2, z_lo: 4; z = z_hi * 4 + z_lo), core: 2. Of those that a mesh axis runs over, the one named last changes fastest.
Arguments:
- queries: bfloat16 [32768, 5120], P(('frame', 'head')), may hold values from -6 to 6, as said below
- keys: bfloat16 [32768, 5120], P(('frame', 'head')), may hold values from -6 to 6, as said below
- values: bfloat16 [32768, 5120], P(('frame', 'head')), may hold values from -6 to 6
- q_gain: float32 [5120], replicated, may hold values from 0.5 to 2
- k_gain: float32 [5120], replicated, may hold values from 0.5 to 2
- block_ids: int32 [32, 8, 8], P('frame'), may hold values from 0 to 23, as said below
- counts: int32 [32, 8], P('frame'), may hold values from 1 to 8, as said below
- anchors: int32 [2], replicated, may hold values from 0 to 31, as said below
Outputs:
- attended: bfloat16 [32768, 5120], P(('frame', 'head'))
The draws below stay inside these ranges and needn't reach their ends.
Inputs may be any that keep to these rules, and one draw needn't show every extreme that they name: `queries`: away from rare tokens, entries are of order one. `keys`: away from rare tokens, entries are of order one. `block_ids`: the 8 entries of one list are different; the first is the query block's own block b. `counts`: every view has a query block that uses all 8 listed blocks. `anchors`: the 2 anchor ids are different; one of them is the last view, 31.
All inputs are finite; a program needn't handle non-finite values.
Results may differ from the reference program's by a relative error of at most 0.012.
The reference program's roundings to bfloat16 on the way (of `q_norm`, `k_norm` and `weights`) count: a program that leaves them out, or rounds other values in their place, can miss the bound.
Values may be sent and summed in bfloat16 or wider, within the bound.
No kernel may reach another device: no remote copies, remote signals or barrier semaphores. Data moves between devices by JAX's collectives and lax.ppermute only.
A program may use at most 128 MiB of HBM per device.

```python
import math
import jax
import jax.numpy as jnp
from jax import lax

D = 5120
HEADS = 40
HD = 128
BLOCK = 128
KB = 8
ANCHORS = 2
VIEW_TOK = 1024
VIEWS = 32
NB = 8
TOKENS = 32768


def draw_queries(key, part):
    key = jax.random.fold_in(key, 21)
    rows = jnp.clip(jax.random.normal(key, (TOKENS, D), jnp.float32), -6.0, 6.0)
    return rows.astype(jnp.bfloat16)


def draw_keys(key, part):
    key = jax.random.fold_in(key, 22)
    rows = jnp.clip(jax.random.normal(key, (TOKENS, D), jnp.float32), -6.0, 6.0)
    return rows.astype(jnp.bfloat16)


def draw_block_ids(key, part):
    key = jax.random.fold_in(key, 11)
    total = (1 + ANCHORS) * NB
    noise = jax.random.randint(key, (VIEWS, NB, total), 0, 4 * NB)
    column = jnp.arange(total, dtype=jnp.int32)
    within = column % NB
    own = jnp.arange(NB, dtype=jnp.int32)
    distance = jnp.abs(within[None, :] - own[:, None])
    score = (4 * distance[None] + noise) * total + column[None, None, :]
    score = jnp.where((column[None, :] == own[:, None])[None], -1, score)
    _, picked = lax.top_k(-score, KB)
    return picked.astype(jnp.int32)


def draw_counts(key, part):
    key = jax.random.fold_in(key, 12)
    first, second, third = jax.random.split(key, 3)
    floor_view = jax.random.randint(first, (VIEWS, 1), 1, KB + 1)
    extra = jax.random.randint(second, (VIEWS, NB), 0, KB // 2 + 1)
    amount = jnp.minimum(floor_view + extra, KB)
    full_block = jax.random.randint(third, (VIEWS,), 0, NB)
    amount = jnp.where(jnp.arange(NB)[None, :] == full_block[:, None], KB, amount)
    return amount.astype(jnp.int32)


def draw_anchors(key, part):
    key = jax.random.fold_in(key, 13)
    first, second = jax.random.split(key, 2)
    others = jax.random.permutation(first, VIEWS - 1)[:ANCHORS].astype(jnp.int32)
    last_slot = jax.random.randint(second, (), 0, ANCHORS)
    places = jnp.arange(ANCHORS, dtype=jnp.int32)
    result = jnp.where(places == last_slot, VIEWS - 1, others)
    return result.astype(jnp.int32)


def levels(key, dims, shards, low, top_value):
    def one(position, parts):
        draws = jax.random.uniform(jax.random.fold_in(jax.random.fold_in(key, 6), position), (parts,), jnp.float32, low / len(shards), top_value / len(shards))
        return jnp.repeat(jnp.exp(draws), dims[position] // parts).reshape((-1,) + (1,) * (len(dims) - position - 1))

    level = one(*shards[0])
    for cut in shards[1:]:
        level = level * one(*cut)
    return level


def centred(own_key, shape, width, most, cuts=(), kind=jnp.bfloat16):
    values = width * jax.random.normal(own_key, shape, jnp.float32)
    if cuts:
        values = values * levels(own_key, shape, cuts, -0.22, 0.18)
    return jnp.clip(values, -most, most).astype(kind)


def setup_inputs(seed: int = 0) -> dict:
    arg_keys = jax.random.split(jax.random.key(seed), 9)
    queries = draw_queries(jax.random.fold_in(arg_keys[8], 71), 0)
    keys = draw_keys(jax.random.fold_in(arg_keys[8], 71), 0)
    values = centred(arg_keys[2], (TOKENS, D), 1.0, 6.0, ((0, 256),))
    q_gain = jnp.clip(jnp.exp(jax.random.uniform(arg_keys[3], (D,), jnp.float32, math.log(0.5), math.log(2.0))), 0.5, 2.0)
    k_gain = jnp.clip(jnp.exp(jax.random.uniform(arg_keys[4], (D,), jnp.float32, math.log(0.5), math.log(2.0))), 0.5, 2.0)
    block_ids = draw_block_ids(jax.random.fold_in(arg_keys[8], 71), 0)
    counts = draw_counts(jax.random.fold_in(arg_keys[8], 71), 0)
    anchors = draw_anchors(jax.random.fold_in(arg_keys[8], 71), 0)
    return {"queries": queries, "keys": keys, "values": values, "q_gain": q_gain, "k_gain": k_gain, "block_ids": block_ids, "counts": counts, "anchors": anchors}


def normalize(rows, gain):
    wide = rows.astype(jnp.float32)
    square = lax.optimization_barrier(jnp.mean(wide * wide, axis=-1, keepdims=True))
    return (wide * lax.rsqrt(square + 1e-06) * gain).astype(jnp.bfloat16)

def reference(queries, keys, values, q_gain, k_gain, block_ids, counts, anchors):
    views = TOKENS // VIEW_TOK
    blocks = VIEW_TOK // BLOCK
    q_norm = normalize(queries, q_gain).reshape(views, VIEW_TOK, HEADS, HD)
    k_norm = normalize(keys, k_gain).reshape(views, VIEW_TOK, HEADS, HD)
    v_rows = values.reshape(views, VIEW_TOK, HEADS, HD)
    anchor_k = jnp.take(k_norm, anchors, axis=0).reshape(ANCHORS * blocks, BLOCK, HEADS, HD)
    anchor_v = jnp.take(v_rows, anchors, axis=0).reshape(ANCHORS * blocks, BLOCK, HEADS, HD)
    scale = 1.0 / math.sqrt(HD)
    slots = jnp.arange(KB, dtype=jnp.int32)

    def one_view(args):
        q_view, k_view, v_view, id_view, count_view = args
        key_blocks = jnp.concatenate([k_view.reshape(blocks, BLOCK, HEADS, HD), anchor_k], axis=0)
        value_blocks = jnp.concatenate([v_view.reshape(blocks, BLOCK, HEADS, HD), anchor_v], axis=0)

        def one_block(inner):
            q_block, id_list, count = inner
            picked_k = key_blocks[id_list].astype(jnp.float32)
            picked_v = value_blocks[id_list].astype(jnp.float32)
            scores = jnp.einsum('qhd,kphd->hqkp', q_block.astype(jnp.float32), picked_k) * scale
            valid = (slots < count)[None, None, :, None]
            scores = jnp.where(valid, scores, -1e+30)
            top = lax.optimization_barrier(jnp.max(scores, axis=(2, 3), keepdims=True))
            expo = jnp.exp(scores - top)
            weights = (expo / lax.optimization_barrier(jnp.sum(expo, axis=(2, 3), keepdims=True))).astype(jnp.bfloat16)
            mixed = jnp.einsum('hqkp,kphd->qhd', weights.astype(jnp.float32), picked_v)
            return mixed.astype(jnp.bfloat16)
        return lax.map(one_block, (q_view.reshape(blocks, BLOCK, HEADS, HD), id_view, count_view))
    result = lax.map(one_view, (q_norm, k_norm, v_rows, block_ids, counts))
    return result.reshape(TOKENS, D)
```

```python
import functools
import math

import jax
import jax.numpy as jnp
from jax import lax
from jax.experimental import pallas as pl
from jax.experimental.pallas import tpu as pltpu
from jax.sharding import Mesh, PartitionSpec as P

HD = 128
BLOCK = 128
LISTED = 8
PLANES = 8
SHARE = 4
PER = SHARE + 1
TAIL = 16
SLOTS = 48
AXES = ("zl", "x", "c", "zh", "y")
PLANE = ("zl", "zh")
EVERY = ("zl", "zh", "y")
VMEM = 56 << 20
HALF = 32 << 20
ANY = pl.BlockSpec(memory_space=pl.ANY)
SMEM = pl.BlockSpec(memory_space=pltpu.SMEM)
F32 = jnp.float32
BF16 = jnp.bfloat16


def norm_kernel(q_ref, k_ref, v_ref, qg_ref, kg_ref, ids_ref, cnt_ref, q_out, kv_out, five_out):
    step, rows = pl.program_id(0), q_ref.shape[0]

    def normed(x_ref, g_ref):
        wide = x_ref[...].astype(F32)
        square = jnp.mean(wide * wide, axis=-1, keepdims=True)
        return (wide * lax.rsqrt(square + 1e-06) * g_ref[...]).astype(BF16)

    def place(wide, slot, put):
        for plane in range(PLANES):
            for lane in range(PER):
                at = (plane * PER + lane) * HD
                tile = wide[:, at : at + HD]
                if lane < SHARE:
                    put(plane * SHARE + lane, tile)
                else:
                    first = pl.multiple_of(slot * BLOCK + step * rows, 32)
                    five_out[plane, pl.ds(first, rows), :] = tile

    def put_q(head, tile):
        q_out[head] = tile

    def put_k(head, tile):
        kv_out[head, 0] = tile

    def put_v(head, tile):
        kv_out[head, 1] = tile

    place(normed(q_ref, qg_ref), 0, put_q)
    place(normed(k_ref, kg_ref), 1, put_k)
    place(v_ref[...], 2, put_v)

    @pl.when(step == 0)
    def _():
        row = lax.broadcasted_iota(jnp.int32, (TAIL, HD), 0)
        lane = lax.broadcasted_iota(jnp.int32, (TAIL, HD), 1)
        lists = jnp.zeros((TAIL, HD), jnp.int32)
        for b in range(ids_ref.shape[1]):
            for s in range(LISTED):
                lists = jnp.where((row == b) & (lane == s), ids_ref[0, b, s], lists)
            lists = jnp.where((row == b) & (lane == LISTED), cnt_ref[0, b], lists)
        for plane in range(PLANES):
            five_out[plane, 3 * BLOCK : 3 * BLOCK + TAIL, :] = lists.astype(F32).astype(BF16)


def norm_and_place(queries, keys, values, q_gain, k_gain, block_ids, counts):
    rows, width = queries.shape
    step = 32
    mains = PLANES * SHARE
    whole = pl.BlockSpec((step, width), lambda i: (i, 0))
    gain = pl.BlockSpec((1, width), lambda i: (0, 0))
    five_shape = (PLANES, 3 * rows + TAIL, HD)
    return pl.pallas_call(
        norm_kernel,
        grid=(rows // step,),
        in_specs=[whole, whole, whole, gain, gain, SMEM, SMEM],
        out_specs=[
            pl.BlockSpec((mains, step, HD), lambda i: (0, i, 0)),
            pl.BlockSpec((mains, 2, step, HD), lambda i: (0, 0, i, 0)),
            pl.BlockSpec(five_shape, lambda i: (0, 0, 0)),
        ],
        out_shape=[
            jax.ShapeDtypeStruct((mains, rows, HD), BF16),
            jax.ShapeDtypeStruct((mains, 2, rows, HD), BF16),
            jax.ShapeDtypeStruct(five_shape, BF16),
        ],
        compiler_params=pltpu.CompilerParams(vmem_limit_bytes=VMEM),
        name="norm_place",
    )(queries, keys, values, q_gain.reshape(1, -1), k_gain.reshape(1, -1), block_ids, counts)


def join_kernel(main_ref, five_ref, out_ref):
    for plane in range(PLANES):
        for lane in range(PER):
            at = (plane * PER + lane) * HD
            if lane < SHARE:
                out_ref[:, at : at + HD] = main_ref[plane * SHARE + lane]
            else:
                out_ref[:, at : at + HD] = five_ref[plane]


def join(main, five):
    rows = main.shape[1]
    step = 32
    width = PLANES * PER * HD
    return pl.pallas_call(
        join_kernel,
        grid=(rows // step,),
        in_specs=[
            pl.BlockSpec((main.shape[0], step, HD), lambda i: (0, i, 0)),
            pl.BlockSpec((PLANES, step, HD), lambda i: (0, i, 0)),
        ],
        out_specs=pl.BlockSpec((step, width), lambda i: (i, 0)),
        out_shape=jax.ShapeDtypeStruct((rows, width), BF16),
        compiler_params=pltpu.CompilerParams(vmem_limit_bytes=HALF),
        name="join_heads",
    )(main, five)


def attend_items(queries, picks, counts, kv, put):
    factor = math.log2(math.e) / math.sqrt(HD)
    ones = jnp.ones((LISTED * BLOCK, HD), BF16)
    scores, tops = [], []
    for query, pick, count in zip(queries, picks, counts):
        keys = jnp.concatenate([kv[p, 0:BLOCK, :] for p in pick], axis=0)
        raw = lax.dot_general(query(), keys, (((1,), (1,)), ((), ())), preferred_element_type=F32)
        parts = []
        for s in range(LISTED):
            bias = jnp.where(s < count, 0.0, -1e30).astype(F32)
            parts.append(raw[:, s * BLOCK : (s + 1) * BLOCK] * factor + bias)
        scores.append(parts)
        tops.append(jnp.max(functools.reduce(jnp.maximum, parts), axis=-1, keepdims=True))
    for i, pick in enumerate(picks):
        weights = jnp.concatenate([jnp.exp2(part - tops[i]).astype(BF16) for part in scores[i]], axis=1)
        values = jnp.concatenate([kv[p, BLOCK : 2 * BLOCK, :] for p in pick], axis=0)
        mixed = jnp.dot(weights, jnp.concatenate([values, ones], axis=1), preferred_element_type=F32)
        put(i, (mixed[:, :HD] / mixed[:, HD:]).astype(BF16))


def fetch(pairs, sems):
    copies = [pltpu.make_async_copy(src, dst, sems.at[i]) for i, (src, dst) in enumerate(pairs)]
    for copy in copies:
        copy.start()
    for copy in copies:
        copy.wait()


def main_kernel(pos_ref, lists_ref, q_ref, all_ref, own_ref, other_ref, out_ref, kv, sems):
    view, c = pl.program_id(0), pos_ref[2]

    @pl.when(view == 0)
    def _():
        pairs = [(all_ref, kv.at[pl.ds(0, 32)])]
        for a in range(2):
            pairs.append((own_ref.at[a], kv.at[pl.ds(32 + 8 * a + 4 * c, 4)]))
            pairs.append((other_ref.at[a], kv.at[pl.ds(32 + 8 * a + 4 * (1 - c), 4)]))
        fetch(pairs, sems)

    queries, picks, counts = [], [], []
    for b in range(8):
        queries.append(functools.partial(lambda b: q_ref[b], b))
        ids = [lists_ref[view, b, s] for s in range(LISTED)]
        picks.append([jnp.where(j < 8, view * 8 + j, 24 + j) for j in ids])
        counts.append(lists_ref[view, b, LISTED])

    def put(i, block):
        out_ref[i] = block

    attend_items(queries, picks, counts, kv, put)


def attend_main(pos, lists, q_all, kv_all, own, other):
    blocks = pl.BlockSpec((8, BLOCK, HD), lambda v: (v, 0, 0))
    return pl.pallas_call(
        main_kernel,
        grid=(4,),
        in_specs=[SMEM, SMEM, blocks, ANY, ANY, ANY],
        out_specs=blocks,
        out_shape=jax.ShapeDtypeStruct(q_all.shape, BF16),
        scratch_shapes=[pltpu.VMEM((SLOTS, 2 * BLOCK, HD), BF16), pltpu.SemaphoreType.DMA((5,))],
        compiler_params=pltpu.CompilerParams(vmem_limit_bytes=VMEM),
        cost_estimate=pl.CostEstimate(
            flops=32 * 4 * BLOCK * LISTED * BLOCK * HD,
            bytes_accessed=4 * SLOTS * BLOCK * HD,
            transcendentals=32 * BLOCK * LISTED * BLOCK,
        ),
        name="attend_main",
    )(pos, lists, q_all, kv_all, own, other)


def shared_kernel(pos_ref, lists_ref, q_ref, five_ref, pack_ref, *rest):
    y_own, y_anchor = rest[:3], rest[3:6]
    out_ref, kv, sems = rest[6:]
    c, y = pos_ref[2], pos_ref[3]
    pairs = [
        (five_ref.at[:, pl.ds(BLOCK, 2 * BLOCK)], kv.at[pl.ds(0, 8)]),
        (pack_ref, kv.at[pl.ds(8, 4)]),
    ]
    for d in (1, 2, 3):
        pairs.append((y_own[d - 1], kv.at[pl.ds(12 * d, 8)]))
        pairs.append((y_anchor[d - 1], kv.at[pl.ds(12 * d + 8, 4)]))
    fetch(pairs, sems)

    queries, picks, counts = [], [], []
    for i in range(PLANES):
        zl, zh = i // 2, i % 2
        queries.append(functools.partial(lambda i: q_ref[i], i))
        pick = []
        for s in range(LISTED):
            j = lists_ref[zl, 4 * zh + y, s]
            away = lax.rem(lax.rem(j, 4) - y + 4, 4)
            upper = lax.rem(j, 8) // 4
            far = 8 + 2 * lax.rem(upper + c, 2) + j // 8 - 1
            pick.append(12 * away + jnp.where(j < 8, 2 * zl + upper, far))
        picks.append(pick)
        counts.append(lists_ref[zl, 4 * zh + y, LISTED])

    def put(i, block):
        out_ref[i] = block

    attend_items(queries, picks, counts, kv, put)


def attend_shared(pos, lists, five, pack, y_own, y_anchor):
    blocks = pl.BlockSpec((PLANES, BLOCK, HD), lambda i: (0, 0, 0))
    return pl.pallas_call(
        shared_kernel,
        grid=(1,),
        in_specs=[SMEM, SMEM, blocks] + [ANY] * 8,
        out_specs=blocks,
        out_shape=jax.ShapeDtypeStruct((PLANES, BLOCK, HD), BF16),
        scratch_shapes=[pltpu.VMEM((SLOTS, 2 * BLOCK, HD), BF16), pltpu.SemaphoreType.DMA((8,))],
        compiler_params=pltpu.CompilerParams(vmem_limit_bytes=VMEM),
        cost_estimate=pl.CostEstimate(
            flops=8 * 4 * BLOCK * LISTED * BLOCK * HD,
            bytes_accessed=4 * SLOTS * BLOCK * HD,
            transcendentals=8 * BLOCK * LISTED * BLOCK,
        ),
        name="attend_shared",
    )(pos, lists, five, five, pack, *y_own, *y_anchor)


def shifted(x, axis, size, by):
    return lax.ppermute(x, axis, [((i + by) % size, i) for i in range(size)])


def core_half(by_zl, at_zl, at_c):
    c = lax.axis_index("c")
    mine = jnp.stack([lax.dynamic_index_in_dim(by_zl, at_zl[a], 0, keepdims=False) for a in range(2)], axis=1)
    kept = lax.dynamic_index_in_dim(mine, c, 0, keepdims=False)
    sent = lax.dynamic_index_in_dim(mine, 1 - c, 0, keepdims=False)
    here = (at_c == c).reshape((2,) + (1,) * (kept.ndim - 1))
    return jnp.where(here, kept, shifted(sent, "c", 2, 1))


def along_x(half):
    return [half] + [shifted(half, "x", 4, by) for by in (1, 2, 3)]


def both_halves(others, at_x):
    away = ((at_x - lax.axis_index("x")) % 4).reshape((2,) + (1,) * (others[0].ndim - 1))
    own = jnp.where(
        away < 2,
        jnp.where(away == 0, others[0], others[1]),
        jnp.where(away == 2, others[2], others[3]),
    )
    return own, shifted(own, "c", 2, 1)


def shards(queries, keys, values, q_gain, k_gain, block_ids, counts, anchors):
    at_zl, at_x, at_c = anchors // 8, (anchors // 2) % 4, anchors % 2
    pos = jnp.stack([lax.axis_index(axis) for axis in ("zl", "zh", "c", "y")])

    q_rows, kv_rows, five = norm_and_place(queries, keys, values, q_gain, k_gain, block_ids, counts)
    five = lax.all_to_all(five, PLANE, 0, 0, tiled=True)
    five, kv_rows, q_rows = lax.optimization_barrier((five, kv_rows, q_rows))
    kv_all = lax.all_to_all(kv_rows, EVERY, 0, 0, tiled=True).reshape(32, 2 * BLOCK, HD)

    lists = five.reshape(4, 2, -1, HD)[:, 0, 3 * BLOCK : 3 * BLOCK + 8, : LISTED + 1].astype(jnp.int32)
    kv_five = five[:, BLOCK : 3 * BLOCK]
    y_own = [shifted(kv_five, "y", 4, by) for by in (1, 2, 3)]
    half = core_half(kv_five.reshape(4, 2, 2 * BLOCK, HD), at_zl, at_c)
    pack = jnp.concatenate(both_halves(along_x(half), at_x), axis=0)
    kv_all, q_rows, pack, *y_own = lax.optimization_barrier((kv_all, q_rows, pack, *y_own))
    q_all = lax.all_to_all(q_rows, EVERY, 0, 0, tiled=True)

    others = along_x(core_half(kv_all.reshape(4, 2, 4, 2 * BLOCK, HD), at_zl, at_c))
    y_anchor = [shifted(pack, "y", 4, by) for by in (1, 2, 3)]
    shared = attend_shared(pos, lists, five, pack, y_own, y_anchor)
    shared, q_all, *others = lax.optimization_barrier((shared, q_all, *others))
    shared = lax.all_to_all(shared, PLANE, 0, 0, tiled=True)
    own, other = both_halves(others, at_x)
    mixed = attend_main(pos, lists, q_all, kv_all, own, other)
    main = lax.all_to_all(mixed, EVERY, 0, 0, tiled=True)
    return join(main, shared)


def solution(mesh):
    fine = Mesh(mesh.devices.reshape(4, 4, 2, 2, 4), AXES)
    tokens = P(AXES, None)
    frame = ("zl", "x", "c")
    placed = (tokens, tokens, tokens, P(), P(), P(frame, None, None), P(frame, None), P())
    return jax.shard_map(shards, mesh=fine, in_specs=placed, out_specs=tokens, check_vma=False)
```

```python
import functools
import math

import jax
import jax.numpy as jnp
from jax import lax
from jax.experimental import pallas as pl
from jax.experimental.pallas import tpu as pltpu
from jax.sharding import Mesh, PartitionSpec as P

HD = 128
BLOCK = 128
LISTED = 8
PLANES = 8
SHARE = 4
PER = SHARE + 1
TAIL = 16
SLOTS = 48
AXES = ("zl", "x", "c", "zh", "y")
PLANE = ("zl", "zh")
EVERY = ("zl", "zh", "y")
VMEM = 56 << 20
HALF = 32 << 20
ANY = pl.BlockSpec(memory_space=pl.ANY)
SMEM = pl.BlockSpec(memory_space=pltpu.SMEM)
F32 = jnp.float32
BF16 = jnp.bfloat16


def inverse(x_ref):
    wide = x_ref[...].astype(F32)
    square = jnp.mean(wide * wide, axis=-1, keepdims=True)
    return lax.rsqrt(square + 1e-06)


def normed(x_ref, scale, g_ref, head):
    at = slice(head * HD, (head + 1) * HD)
    return (x_ref[:, at].astype(F32) * scale * g_ref[:, at]).astype(BF16)


def shared_rows_kernel(q_ref, k_ref, v_ref, qg_ref, kg_ref, ids_ref, cnt_ref, out_ref):
    step, rows = pl.program_id(0), q_ref.shape[0]
    q_scale, k_scale = inverse(q_ref), inverse(k_ref)
    for plane in range(PLANES):
        head = plane * PER + SHARE
        tiles = (
            normed(q_ref, q_scale, qg_ref, head),
            normed(k_ref, k_scale, kg_ref, head),
            v_ref[:, head * HD : (head + 1) * HD],
        )
        for slot, tile in enumerate(tiles):
            out_ref[plane, pl.ds(pl.multiple_of(slot * BLOCK + step * rows, 32), rows), :] = tile

    @pl.when(step == 0)
    def _():
        row = lax.broadcasted_iota(jnp.int32, (TAIL, HD), 0)
        lane = lax.broadcasted_iota(jnp.int32, (TAIL, HD), 1)
        lists = jnp.zeros((TAIL, HD), jnp.int32)
        for b in range(8):
            for s in range(LISTED):
                lists = jnp.where((row == b) & (lane == s), ids_ref[0, b, s], lists)
            lists = jnp.where((row == b) & (lane == LISTED), cnt_ref[0, b], lists)
        for plane in range(PLANES):
            out_ref[plane, 3 * BLOCK : 3 * BLOCK + TAIL, :] = lists.astype(F32).astype(BF16)


def own_rows_kernel(q_ref, k_ref, v_ref, qg_ref, kg_ref, q_out, kv_out):
    q_scale, k_scale = inverse(q_ref), inverse(k_ref)
    for plane in range(PLANES):
        for lane in range(SHARE):
            to, head = plane * SHARE + lane, plane * PER + lane
            q_out[to] = normed(q_ref, q_scale, qg_ref, head)
            kv_out[to, 0] = normed(k_ref, k_scale, kg_ref, head)
            kv_out[to, 1] = v_ref[:, head * HD : (head + 1) * HD]


def placed(queries, keys, values, q_gain, k_gain, block_ids, counts):
    rows, width = queries.shape
    step = 32
    heads = PLANES * SHARE
    whole = pl.BlockSpec((step, width), lambda i: (i, 0))
    gain = pl.BlockSpec((1, width), lambda i: (0, 0))
    shared = (PLANES, 3 * rows + TAIL, HD)
    inputs = (queries, keys, values, q_gain.reshape(1, -1), k_gain.reshape(1, -1))
    five = pl.pallas_call(
        shared_rows_kernel,
        grid=(rows // step,),
        in_specs=[whole, whole, whole, gain, gain, SMEM, SMEM],
        out_specs=pl.BlockSpec(shared, lambda i: (0, 0, 0)),
        out_shape=jax.ShapeDtypeStruct(shared, BF16),
        compiler_params=pltpu.CompilerParams(vmem_limit_bytes=VMEM),
        name="shared_rows",
    )(*inputs, block_ids, counts)
    q_rows, kv_rows = pl.pallas_call(
        own_rows_kernel,
        grid=(rows // step,),
        in_specs=[whole, whole, whole, gain, gain],
        out_specs=[
            pl.BlockSpec((heads, step, HD), lambda i: (0, i, 0)),
            pl.BlockSpec((heads, 2, step, HD), lambda i: (0, 0, i, 0)),
        ],
        out_shape=[
            jax.ShapeDtypeStruct((heads, rows, HD), BF16),
            jax.ShapeDtypeStruct((heads, 2, rows, HD), BF16),
        ],
        compiler_params=pltpu.CompilerParams(vmem_limit_bytes=VMEM),
        name="own_rows",
    )(*inputs)
    return five, q_rows, kv_rows


def join_kernel(main_ref, five_ref, out_ref):
    for plane in range(PLANES):
        for lane in range(PER):
            at = (plane * PER + lane) * HD
            if lane < SHARE:
                out_ref[:, at : at + HD] = main_ref[plane * SHARE + lane]
            else:
                out_ref[:, at : at + HD] = five_ref[plane]


def join(main, five):
    rows = main.shape[1]
    step = 32
    width = PLANES * PER * HD
    return pl.pallas_call(
        join_kernel,
        grid=(rows // step,),
        in_specs=[
            pl.BlockSpec((main.shape[0], step, HD), lambda i: (0, i, 0)),
            pl.BlockSpec((PLANES, step, HD), lambda i: (0, i, 0)),
        ],
        out_specs=pl.BlockSpec((step, width), lambda i: (i, 0)),
        out_shape=jax.ShapeDtypeStruct((rows, width), BF16),
        compiler_params=pltpu.CompilerParams(vmem_limit_bytes=HALF),
        name="join_heads",
    )(main, five)


def attend_items(queries, picks, counts, kv, put):
    factor = math.log2(math.e) / math.sqrt(HD)
    ones = jnp.ones((LISTED * BLOCK, HD), BF16)
    scores, tops = [], []
    for query, pick, count in zip(queries, picks, counts):
        keys = jnp.concatenate([kv[p, 0:BLOCK, :] for p in pick], axis=0)
        raw = lax.dot_general(query(), keys, (((1,), (1,)), ((), ())), preferred_element_type=F32)
        parts = []
        for s in range(LISTED):
            bias = jnp.where(s < count, 0.0, -1e30).astype(F32)
            parts.append(raw[:, s * BLOCK : (s + 1) * BLOCK] * factor + bias)
        scores.append(parts)
        tops.append(jnp.max(functools.reduce(jnp.maximum, parts), axis=-1, keepdims=True))
    for i, pick in enumerate(picks):
        weights = jnp.concatenate([jnp.exp2(part - tops[i]).astype(BF16) for part in scores[i]], axis=1)
        values = jnp.concatenate([kv[p, BLOCK : 2 * BLOCK, :] for p in pick], axis=0)
        mixed = jnp.dot(weights, jnp.concatenate([values, ones], axis=1), preferred_element_type=F32)
        put(i, (mixed[:, :HD] / mixed[:, HD:]).astype(BF16))


def fetch(pairs, sems):
    copies = [pltpu.make_async_copy(src, dst, sems.at[i]) for i, (src, dst) in enumerate(pairs)]
    for copy in copies:
        copy.start()
    for copy in copies:
        copy.wait()


def main_kernel(pos_ref, lists_ref, q_ref, all_ref, own_ref, other_ref, out_ref, kv, sems):
    view, c = pl.program_id(0), pos_ref[2]

    @pl.when(view == 0)
    def _():
        pairs = [(all_ref, kv.at[pl.ds(0, 32)])]
        for a in range(2):
            pairs.append((own_ref.at[a], kv.at[pl.ds(32 + 8 * a + 4 * c, 4)]))
            pairs.append((other_ref.at[a], kv.at[pl.ds(32 + 8 * a + 4 * (1 - c), 4)]))
        fetch(pairs, sems)

    queries, picks, counts = [], [], []
    for b in range(8):
        queries.append(functools.partial(lambda b: q_ref[b], b))
        ids = [lists_ref[view, b, s] for s in range(LISTED)]
        picks.append([jnp.where(j < 8, view * 8 + j, 24 + j) for j in ids])
        counts.append(lists_ref[view, b, LISTED])

    def put(i, block):
        out_ref[i] = block

    attend_items(queries, picks, counts, kv, put)


def attend_main(pos, lists, q_all, kv_all, own, other):
    blocks = pl.BlockSpec((8, BLOCK, HD), lambda v: (v, 0, 0))
    return pl.pallas_call(
        main_kernel,
        grid=(4,),
        in_specs=[SMEM, SMEM, blocks, ANY, ANY, ANY],
        out_specs=blocks,
        out_shape=jax.ShapeDtypeStruct(q_all.shape, BF16),
        scratch_shapes=[pltpu.VMEM((SLOTS, 2 * BLOCK, HD), BF16), pltpu.SemaphoreType.DMA((5,))],
        compiler_params=pltpu.CompilerParams(vmem_limit_bytes=VMEM),
        cost_estimate=pl.CostEstimate(
            flops=32 * 4 * BLOCK * LISTED * BLOCK * HD,
            bytes_accessed=4 * SLOTS * BLOCK * HD,
            transcendentals=32 * BLOCK * LISTED * BLOCK,
        ),
        name="attend_main",
    )(pos, lists, q_all, kv_all, own, other)


def shared_kernel(pos_ref, lists_ref, five_ref, *rest):
    got, near_ref, far_ref = rest[:3], rest[3], rest[4]
    outs, q, kv, sems = rest[5:9], rest[9], rest[10], rest[11]
    c, y = pos_ref[2], pos_ref[3]
    pairs = [(near_ref, kv.at[pl.ds(8, 8)]), (far_ref, kv.at[pl.ds(16, 8)])]
    for d in range(4):
        mine = five_ref.at[pl.ds(2 * y, 2)] if d == 0 else got[d - 1]
        pairs.append((mine.at[:, pl.ds(0, BLOCK)], q.at[pl.ds(2 * d, 2)]))
        pairs.append((mine.at[:, pl.ds(BLOCK, 2 * BLOCK)], kv.at[pl.ds(2 * d, 2)]))
    fetch(pairs, sems)

    queries, picks, counts = [], [], []
    for i in range(8):
        row = 4 * (i % 2) + lax.rem(y + i // 2, 4)
        queries.append(functools.partial(lambda i: q[i], i))
        pick = []
        for s in range(LISTED):
            j = lists_ref[y, row, s]
            away = lax.rem(lax.rem(j, 4) - y + 4, 4)
            upper = lax.rem(j, 8) // 4
            far = 8 + 8 * lax.rem(upper + c, 2) + 2 * away + j // 8 - 1
            pick.append(jnp.where(j < 8, 2 * away + upper, far))
        picks.append(pick)
        counts.append(lists_ref[y, row, LISTED])

    def put(i, block):
        outs[i // 2][i % 2] = block

    attend_items(queries, picks, counts, kv, put)


def attend_shared(pos, lists, five, got, near, far):
    blocks = pl.BlockSpec((2, BLOCK, HD), lambda i: (0, 0, 0))
    return pl.pallas_call(
        shared_kernel,
        grid=(1,),
        in_specs=[SMEM, SMEM] + [ANY] * 6,
        out_specs=[blocks] * SHARE,
        out_shape=[jax.ShapeDtypeStruct((2, BLOCK, HD), BF16)] * SHARE,
        scratch_shapes=[
            pltpu.VMEM((8, BLOCK, HD), BF16),
            pltpu.VMEM((24, 2 * BLOCK, HD), BF16),
            pltpu.SemaphoreType.DMA((10,)),
        ],
        compiler_params=pltpu.CompilerParams(vmem_limit_bytes=VMEM),
        cost_estimate=pl.CostEstimate(
            flops=8 * 4 * BLOCK * LISTED * BLOCK * HD,
            bytes_accessed=4 * 24 * BLOCK * HD,
            transcendentals=8 * BLOCK * LISTED * BLOCK,
        ),
        name="attend_shared",
    )(pos, lists, five, *got, near, far)


def shifted(x, axis, size, by):
    return lax.ppermute(x, axis, [((i + by) % size, i) for i in range(size)])


def core_half(by_zl, at_zl, at_c):
    c = lax.axis_index("c")
    mine = jnp.stack([lax.dynamic_index_in_dim(by_zl, at_zl[a], 0, keepdims=False) for a in range(2)], axis=1)
    kept = lax.dynamic_index_in_dim(mine, c, 0, keepdims=False)
    sent = lax.dynamic_index_in_dim(mine, 1 - c, 0, keepdims=False)
    here = (at_c == c).reshape((2,) + (1,) * (kept.ndim - 1))
    return jnp.where(here, kept, shifted(sent, "c", 2, 1))


def along_x(half):
    return [half] + [shifted(half, "x", 4, by) for by in (1, 2, 3)]


def true_half(others, at_x):
    away = ((at_x - lax.axis_index("x")) % 4).reshape((2,) + (1,) * (others[0].ndim - 1))
    return jnp.where(
        away < 2,
        jnp.where(away == 0, others[0], others[1]),
        jnp.where(away == 2, others[2], others[3]),
    )


def shards(queries, keys, values, q_gain, k_gain, block_ids, counts, anchors):
    at_zl, at_x, at_c = anchors // 8, (anchors // 2) % 4, anchors % 2
    pos = jnp.stack([lax.axis_index(axis) for axis in ("zl", "zh", "c", "y")])

    five, q_rows, kv_rows = placed(queries, keys, values, q_gain, k_gain, block_ids, counts)
    five = lax.all_to_all(five, PLANE, 0, 0, tiled=True)
    five, kv_rows, q_rows = lax.optimization_barrier((five, kv_rows, q_rows))
    kv_all = lax.all_to_all(kv_rows, EVERY, 0, 0, tiled=True).reshape(32, 2 * BLOCK, HD)

    y = lax.axis_index("y")
    by_view = five.reshape(4, 2, -1, HD)
    lists = by_view[:, 0, 3 * BLOCK : 3 * BLOCK + 8, : LISTED + 1].astype(jnp.int32)
    half = core_half(by_view[:, :, BLOCK : 3 * BLOCK], at_zl, at_c)
    half = true_half(along_x(half), at_x)
    got = []
    for by in (1, 2, 3):
        view = lax.dynamic_index_in_dim(by_view[:, :, : 3 * BLOCK], (y - by) % 4, 0, keepdims=False)
        got.append(shifted(view, "y", 4, by))
    near = jnp.concatenate([half] + [shifted(half, "y", 4, by) for by in (1, 2, 3)], axis=0)
    far = shifted(near, "c", 2, 1)
    kv_all, q_rows, near, far, *got = lax.optimization_barrier((kv_all, q_rows, near, far, *got))
    q_all = lax.all_to_all(q_rows, EVERY, 0, 0, tiled=True)

    half = core_half(kv_all.reshape(4, 2, 4, 2 * BLOCK, HD), at_zl, at_c)
    half, near = lax.optimization_barrier((half, near))
    others = along_x(half)
    parts = attend_shared(pos, lists, five, got, near, far)
    back = jnp.stack([parts[0]] + [shifted(parts[d], "y", 4, -d) for d in (3, 2, 1)])
    shared = lax.dynamic_slice_in_dim(jnp.concatenate([back, back]), 4 - y, 4, 0).reshape(PLANES, BLOCK, HD)
    shared, q_all = lax.optimization_barrier((shared, q_all))
    home = lax.all_to_all(shared, PLANE, 0, 0, tiled=True)
    shared, q_all, *others = lax.optimization_barrier((shared, q_all, *others))
    own = true_half(others, at_x)
    other = shifted(own, "c", 2, 1)
    mixed = attend_main(pos, lists, q_all, kv_all, own, other)
    main = lax.all_to_all(mixed, EVERY, 0, 0, tiled=True)
    return join(main, home)


def solution(mesh):
    fine = Mesh(mesh.devices.reshape(4, 4, 2, 2, 4), AXES)
    tokens = P(AXES, None)
    frame = ("zl", "x", "c")
    placed = (tokens, tokens, tokens, P(), P(), P(frame, None, None), P(frame, None), P())
    return jax.shard_map(shards, mesh=fine, in_specs=placed, out_specs=tokens, check_vma=False)
```

```python
import functools
import math

import jax
import jax.numpy as jnp
from jax import lax
from jax.experimental import pallas as pl
from jax.experimental.pallas import tpu as pltpu
from jax.sharding import Mesh, PartitionSpec as P

HD = 128
BLOCK = 128
LISTED = 8
PLANES = 8
SHARE = 4
PER = SHARE + 1
TAIL = 16
SLOTS = 48
AXES = ("zl", "x", "c", "zh", "y")
PLANE = ("zl", "zh")
EVERY = ("zl", "zh", "y")
VMEM = 56 << 20
HALF = 32 << 20
ANY = pl.BlockSpec(memory_space=pl.ANY)
SMEM = pl.BlockSpec(memory_space=pltpu.SMEM)
F32 = jnp.float32
BF16 = jnp.bfloat16


def inverse(x_ref):
    wide = x_ref[...].astype(F32)
    square = jnp.mean(wide * wide, axis=-1, keepdims=True)
    return lax.rsqrt(square + 1e-06)


def normed(x_ref, scale, g_ref, head):
    at = slice(head * HD, (head + 1) * HD)
    return (x_ref[:, at].astype(F32) * scale * g_ref[:, at]).astype(BF16)


def shared_rows_kernel(q_ref, k_ref, v_ref, qg_ref, kg_ref, ids_ref, cnt_ref, out_ref):
    step, rows = pl.program_id(0), q_ref.shape[0]
    q_scale, k_scale = inverse(q_ref), inverse(k_ref)
    for plane in range(PLANES):
        head = plane * PER + SHARE
        tiles = (
            normed(q_ref, q_scale, qg_ref, head),
            normed(k_ref, k_scale, kg_ref, head),
            v_ref[:, head * HD : (head + 1) * HD],
        )
        for slot, tile in enumerate(tiles):
            out_ref[plane, pl.ds(pl.multiple_of(slot * BLOCK + step * rows, 32), rows), :] = tile

    @pl.when(step == 0)
    def _():
        row = lax.broadcasted_iota(jnp.int32, (TAIL, HD), 0)
        lane = lax.broadcasted_iota(jnp.int32, (TAIL, HD), 1)
        lists = jnp.zeros((TAIL, HD), jnp.int32)
        for b in range(8):
            for s in range(LISTED):
                lists = jnp.where((row == b) & (lane == s), ids_ref[0, b, s], lists)
            lists = jnp.where((row == b) & (lane == LISTED), cnt_ref[0, b], lists)
        for plane in range(PLANES):
            out_ref[plane, 3 * BLOCK : 3 * BLOCK + TAIL, :] = lists.astype(F32).astype(BF16)


def own_rows_kernel(q_ref, k_ref, v_ref, qg_ref, kg_ref, q_out, kv_out):
    q_scale, k_scale = inverse(q_ref), inverse(k_ref)
    for plane in range(PLANES):
        for lane in range(SHARE):
            to, head = plane * SHARE + lane, plane * PER + lane
            q_out[to] = normed(q_ref, q_scale, qg_ref, head)
            kv_out[to, 0] = normed(k_ref, k_scale, kg_ref, head)
            kv_out[to, 1] = v_ref[:, head * HD : (head + 1) * HD]


def placed(queries, keys, values, q_gain, k_gain, block_ids, counts):
    rows, width = queries.shape
    step = 32
    heads = PLANES * SHARE
    whole = pl.BlockSpec((step, width), lambda i: (i, 0))
    gain = pl.BlockSpec((1, width), lambda i: (0, 0))
    shared = (PLANES, 3 * rows + TAIL, HD)
    inputs = (queries, keys, values, q_gain.reshape(1, -1), k_gain.reshape(1, -1))
    five = pl.pallas_call(
        shared_rows_kernel,
        grid=(rows // step,),
        in_specs=[whole, whole, whole, gain, gain, SMEM, SMEM],
        out_specs=pl.BlockSpec(shared, lambda i: (0, 0, 0)),
        out_shape=jax.ShapeDtypeStruct(shared, BF16),
        compiler_params=pltpu.CompilerParams(vmem_limit_bytes=VMEM),
        name="shared_rows",
    )(*inputs, block_ids, counts)
    q_rows, kv_rows = pl.pallas_call(
        own_rows_kernel,
        grid=(rows // step,),
        in_specs=[whole, whole, whole, gain, gain],
        out_specs=[
            pl.BlockSpec((heads, step, HD), lambda i: (0, i, 0)),
            pl.BlockSpec((heads, 2, step, HD), lambda i: (0, 0, i, 0)),
        ],
        out_shape=[
            jax.ShapeDtypeStruct((heads, rows, HD), BF16),
            jax.ShapeDtypeStruct((heads, 2, rows, HD), BF16),
        ],
        compiler_params=pltpu.CompilerParams(vmem_limit_bytes=VMEM),
        name="own_rows",
    )(*inputs)
    return five, q_rows, kv_rows


def join_kernel(main_ref, five_ref, out_ref):
    for plane in range(PLANES):
        for lane in range(PER):
            at = (plane * PER + lane) * HD
            if lane < SHARE:
                out_ref[:, at : at + HD] = main_ref[plane * SHARE + lane]
            else:
                out_ref[:, at : at + HD] = five_ref[plane]


def join(main, five):
    rows = main.shape[1]
    step = 32
    width = PLANES * PER * HD
    return pl.pallas_call(
        join_kernel,
        grid=(rows // step,),
        in_specs=[
            pl.BlockSpec((main.shape[0], step, HD), lambda i: (0, i, 0)),
            pl.BlockSpec((PLANES, step, HD), lambda i: (0, i, 0)),
        ],
        out_specs=pl.BlockSpec((step, width), lambda i: (i, 0)),
        out_shape=jax.ShapeDtypeStruct((rows, width), BF16),
        compiler_params=pltpu.CompilerParams(vmem_limit_bytes=HALF),
        name="join_heads",
    )(main, five)


def attend_items(queries, picks, counts, kv, put):
    factor = math.log2(math.e) / math.sqrt(HD)
    ones = jnp.ones((LISTED * BLOCK, HD), BF16)
    scores, tops = [], []
    for query, pick, count in zip(queries, picks, counts):
        keys = jnp.concatenate([kv[p, 0:BLOCK, :] for p in pick], axis=0)
        raw = lax.dot_general(query(), keys, (((1,), (1,)), ((), ())), preferred_element_type=F32)
        parts = []
        for s in range(LISTED):
            bias = jnp.where(s < count, 0.0, -1e30).astype(F32)
            parts.append(raw[:, s * BLOCK : (s + 1) * BLOCK] * factor + bias)
        scores.append(parts)
        tops.append(jnp.max(functools.reduce(jnp.maximum, parts), axis=-1, keepdims=True))
    for i, pick in enumerate(picks):
        weights = jnp.concatenate([jnp.exp2(part - tops[i]).astype(BF16) for part in scores[i]], axis=1)
        values = jnp.concatenate([kv[p, BLOCK : 2 * BLOCK, :] for p in pick], axis=0)
        mixed = jnp.dot(weights, jnp.concatenate([values, ones], axis=1), preferred_element_type=F32)
        put(i, (mixed[:, :HD] / mixed[:, HD:]).astype(BF16))


def fetch(pairs, sems):
    copies = [pltpu.make_async_copy(src, dst, sems.at[i]) for i, (src, dst) in enumerate(pairs)]
    for copy in copies:
        copy.start()
    for copy in copies:
        copy.wait()


def main_kernel(pos_ref, lists_ref, q_ref, all_ref, own_ref, other_ref, out_ref, kv, sems):
    view, c = pl.program_id(0), pos_ref[2]

    @pl.when(view == 0)
    def _():
        pairs = [(all_ref, kv.at[pl.ds(0, 32)])]
        for a in range(2):
            pairs.append((own_ref.at[a], kv.at[pl.ds(32 + 8 * a + 4 * c, 4)]))
            pairs.append((other_ref.at[a], kv.at[pl.ds(32 + 8 * a + 4 * (1 - c), 4)]))
        fetch(pairs, sems)

    queries, picks, counts = [], [], []
    for b in range(8):
        queries.append(functools.partial(lambda b: q_ref[b], b))
        ids = [lists_ref[view, b, s] for s in range(LISTED)]
        picks.append([jnp.where(j < 8, view * 8 + j, 24 + j) for j in ids])
        counts.append(lists_ref[view, b, LISTED])

    def put(i, block):
        out_ref[i] = block

    attend_items(queries, picks, counts, kv, put)


def attend_main(pos, lists, q_all, kv_all, own, other):
    blocks = pl.BlockSpec((8, BLOCK, HD), lambda v: (v, 0, 0))
    return pl.pallas_call(
        main_kernel,
        grid=(4,),
        in_specs=[SMEM, SMEM, blocks, ANY, ANY, ANY],
        out_specs=blocks,
        out_shape=jax.ShapeDtypeStruct(q_all.shape, BF16),
        scratch_shapes=[pltpu.VMEM((SLOTS, 2 * BLOCK, HD), BF16), pltpu.SemaphoreType.DMA((5,))],
        compiler_params=pltpu.CompilerParams(vmem_limit_bytes=HALF),
        cost_estimate=pl.CostEstimate(
            flops=32 * 4 * BLOCK * LISTED * BLOCK * HD,
            bytes_accessed=4 * SLOTS * BLOCK * HD,
            transcendentals=32 * BLOCK * LISTED * BLOCK,
        ),
        name="attend_main",
    )(pos, lists, q_all, kv_all, own, other)


def shared_kernel(pos_ref, lists_ref, five_ref, *rest):
    got, near_ref, far_ref = rest[:3], rest[3], rest[4]
    outs, q, kv, sems = rest[5:9], rest[9], rest[10], rest[11]
    c, y = pos_ref[2], pos_ref[3]
    pairs = [(near_ref, kv.at[pl.ds(8, 8)]), (far_ref, kv.at[pl.ds(16, 8)])]
    for d in range(4):
        mine = five_ref.at[pl.ds(2 * y, 2)] if d == 0 else got[d - 1]
        pairs.append((mine.at[:, pl.ds(0, BLOCK)], q.at[pl.ds(2 * d, 2)]))
        pairs.append((mine.at[:, pl.ds(BLOCK, 2 * BLOCK)], kv.at[pl.ds(2 * d, 2)]))
    fetch(pairs, sems)

    queries, picks, counts = [], [], []
    for i in range(8):
        row = 4 * (i % 2) + lax.rem(y + i // 2, 4)
        queries.append(functools.partial(lambda i: q[i], i))
        pick = []
        for s in range(LISTED):
            j = lists_ref[y, row, s]
            away = lax.rem(lax.rem(j, 4) - y + 4, 4)
            upper = lax.rem(j, 8) // 4
            far = 8 + 8 * lax.rem(upper + c, 2) + 2 * away + j // 8 - 1
            pick.append(jnp.where(j < 8, 2 * away + upper, far))
        picks.append(pick)
        counts.append(lists_ref[y, row, LISTED])

    def put(i, block):
        outs[i // 2][i % 2] = block

    attend_items(queries, picks, counts, kv, put)


def attend_shared(pos, lists, five, got, near, far):
    blocks = pl.BlockSpec((2, BLOCK, HD), lambda i: (0, 0, 0))
    return pl.pallas_call(
        shared_kernel,
        grid=(1,),
        in_specs=[SMEM, SMEM] + [ANY] * 6,
        out_specs=[blocks] * SHARE,
        out_shape=[jax.ShapeDtypeStruct((2, BLOCK, HD), BF16)] * SHARE,
        scratch_shapes=[
            pltpu.VMEM((8, BLOCK, HD), BF16),
            pltpu.VMEM((24, 2 * BLOCK, HD), BF16),
            pltpu.SemaphoreType.DMA((10,)),
        ],
        compiler_params=pltpu.CompilerParams(vmem_limit_bytes=HALF),
        cost_estimate=pl.CostEstimate(
            flops=8 * 4 * BLOCK * LISTED * BLOCK * HD,
            bytes_accessed=4 * 24 * BLOCK * HD,
            transcendentals=8 * BLOCK * LISTED * BLOCK,
        ),
        name="attend_shared",
    )(pos, lists, five, *got, near, far)


def shifted(x, axis, size, by):
    return lax.ppermute(x, axis, [((i + by) % size, i) for i in range(size)])


def ring_kernel(me_ref, *rest):
    parts, out_ref = rest[:-1], rest[-1]
    for r, part in enumerate(parts):
        out_ref[lax.rem(me_ref[0] - r + len(parts), len(parts))] = part[...]


def ordered(me, parts, name):
    count, shape = len(parts), parts[0].shape
    zeros = (0,) * len(shape)
    return pl.pallas_call(
        ring_kernel,
        grid=(1,),
        in_specs=[SMEM] + [pl.BlockSpec(shape, lambda i: zeros)] * count,
        out_specs=pl.BlockSpec((count, *shape), lambda i: (0, *zeros)),
        out_shape=jax.ShapeDtypeStruct((count, *shape), BF16),
        compiler_params=pltpu.CompilerParams(vmem_limit_bytes=HALF),
        name=name,
    )(me.reshape(1), *parts)


def core_half(by_zl, at_zl, at_c):
    c = lax.axis_index("c")
    mine = jnp.stack([lax.dynamic_index_in_dim(by_zl, at_zl[a], 0, keepdims=False) for a in range(2)], axis=1)
    kept = lax.dynamic_index_in_dim(mine, c, 0, keepdims=False)
    sent = lax.dynamic_index_in_dim(mine, 1 - c, 0, keepdims=False)
    here = (at_c == c).reshape((2,) + (1,) * (kept.ndim - 1))
    return jnp.where(here, kept, shifted(sent, "c", 2, 1))


def along_x(half):
    return [half] + [shifted(half, "x", 4, by) for by in (1, 2, 3)]


def true_half(others, at_x):
    away = ((at_x - lax.axis_index("x")) % 4).reshape((2,) + (1,) * (others[0].ndim - 1))
    return jnp.where(
        away < 2,
        jnp.where(away == 0, others[0], others[1]),
        jnp.where(away == 2, others[2], others[3]),
    )


def shards(queries, keys, values, q_gain, k_gain, block_ids, counts, anchors):
    at_zl, at_x, at_c = anchors // 8, (anchors // 2) % 4, anchors % 2
    pos = jnp.stack([lax.axis_index(axis) for axis in ("zl", "zh", "c", "y")])

    five, q_rows, kv_rows = placed(queries, keys, values, q_gain, k_gain, block_ids, counts)
    five = lax.all_to_all(five, PLANE, 0, 0, tiled=True)
    five, kv_rows, q_rows = lax.optimization_barrier((five, kv_rows, q_rows))
    kv_all = lax.all_to_all(kv_rows, EVERY, 0, 0, tiled=True).reshape(32, 2 * BLOCK, HD)

    y = lax.axis_index("y")
    by_view = five.reshape(4, 2, -1, HD)
    lists = by_view[:, 0, 3 * BLOCK : 3 * BLOCK + 8, : LISTED + 1].astype(jnp.int32)
    half = core_half(by_view[:, :, BLOCK : 3 * BLOCK], at_zl, at_c)
    half = true_half(along_x(half), at_x)
    got = []
    for by in (1, 2, 3):
        view = lax.dynamic_index_in_dim(by_view[:, :, : 3 * BLOCK], (y - by) % 4, 0, keepdims=False)
        got.append(shifted(view, "y", 4, by))
    half, *got = lax.optimization_barrier((half, *got))
    near = jnp.concatenate([half] + [shifted(half, "y", 4, by) for by in (1, 2, 3)], axis=0)
    far = shifted(near, "c", 2, 1)
    kv_all, q_rows, near, far, *got = lax.optimization_barrier((kv_all, q_rows, near, far, *got))
    q_all = lax.all_to_all(q_rows, EVERY, 0, 0, tiled=True)

    half = core_half(kv_all.reshape(4, 2, 4, 2 * BLOCK, HD), at_zl, at_c)
    half, near = lax.optimization_barrier((half, near))
    others = along_x(half)
    parts = attend_shared(pos, lists, five, got, near, far)
    shared = [parts[0]] + [shifted(parts[d], "y", 4, -d) for d in (1, 2, 3)]
    shared = ordered(y, shared, "order_views").reshape(PLANES, BLOCK, HD)
    shared, q_all = lax.optimization_barrier((shared, q_all))
    home = lax.all_to_all(shared, PLANE, 0, 0, tiled=True)
    shared, q_all, *others = lax.optimization_barrier((shared, q_all, *others))
    own = true_half(others, at_x)
    other = shifted(own, "c", 2, 1)
    mixed = attend_main(pos, lists, q_all, kv_all, own, other)
    main = lax.all_to_all(mixed, EVERY, 0, 0, tiled=True)
    return join(main, home)


def solution(mesh):
    fine = Mesh(mesh.devices.reshape(4, 4, 2, 2, 4), AXES)
    tokens = P(AXES, None)
    frame = ("zl", "x", "c")
    placed = (tokens, tokens, tokens, P(), P(), P(frame, None, None), P(frame, None), P())
    return jax.shard_map(shards, mesh=fine, in_specs=placed, out_specs=tokens, check_vma=False)
```

```python
import functools
import math

import jax
import jax.numpy as jnp
from jax import lax
from jax.experimental import pallas as pl
from jax.experimental.pallas import tpu as pltpu
from jax.sharding import Mesh, PartitionSpec as P

HD = 128
BLOCK = 128
LISTED = 8
PLANES = 8
SHARE = 4
PER = SHARE + 1
TAIL = 16
SLOTS = 48
AXES = ("zl", "x", "c", "zh", "y")
PLANE = ("zl", "zh")
EVERY = ("zl", "zh", "y")
VMEM = 56 << 20
HALF = 32 << 20
ANY = pl.BlockSpec(memory_space=pl.ANY)
SMEM = pl.BlockSpec(memory_space=pltpu.SMEM)
F32 = jnp.float32
BF16 = jnp.bfloat16


def inverse(x_ref):
    wide = x_ref[...].astype(F32)
    square = jnp.mean(wide * wide, axis=-1, keepdims=True)
    return lax.rsqrt(square + 1e-06)


def normed(x_ref, scale, g_ref, head):
    at = slice(head * HD, (head + 1) * HD)
    return (x_ref[:, at].astype(F32) * scale * g_ref[:, at]).astype(BF16)


def shared_rows_kernel(q_ref, k_ref, v_ref, qg_ref, kg_ref, ids_ref, cnt_ref, out_ref):
    step, rows = pl.program_id(0), q_ref.shape[0]
    q_scale, k_scale = inverse(q_ref), inverse(k_ref)
    for plane in range(PLANES):
        head = plane * PER + SHARE
        tiles = (
            normed(q_ref, q_scale, qg_ref, head),
            normed(k_ref, k_scale, kg_ref, head),
            v_ref[:, head * HD : (head + 1) * HD],
        )
        for slot, tile in enumerate(tiles):
            out_ref[plane, pl.ds(pl.multiple_of(slot * BLOCK + step * rows, 32), rows), :] = tile

    @pl.when(step == 0)
    def _():
        row = lax.broadcasted_iota(jnp.int32, (TAIL, HD), 0)
        lane = lax.broadcasted_iota(jnp.int32, (TAIL, HD), 1)
        lists = jnp.zeros((TAIL, HD), jnp.int32)
        for b in range(8):
            for s in range(LISTED):
                lists = jnp.where((row == b) & (lane == s), ids_ref[0, b, s], lists)
            lists = jnp.where((row == b) & (lane == LISTED), cnt_ref[0, b], lists)
        for plane in range(PLANES):
            out_ref[plane, 3 * BLOCK : 3 * BLOCK + TAIL, :] = lists.astype(F32).astype(BF16)


def own_rows_kernel(q_ref, k_ref, v_ref, qg_ref, kg_ref, q_out, kv_out):
    q_scale, k_scale = inverse(q_ref), inverse(k_ref)
    for plane in range(PLANES):
        for lane in range(SHARE):
            to, head = plane * SHARE + lane, plane * PER + lane
            q_out[to] = normed(q_ref, q_scale, qg_ref, head)
            kv_out[to, 0] = normed(k_ref, k_scale, kg_ref, head)
            kv_out[to, 1] = v_ref[:, head * HD : (head + 1) * HD]


def placed(queries, keys, values, q_gain, k_gain, block_ids, counts):
    rows, width = queries.shape
    step = 32
    heads = PLANES * SHARE
    whole = pl.BlockSpec((step, width), lambda i: (i, 0))
    gain = pl.BlockSpec((1, width), lambda i: (0, 0))
    shared = (PLANES, 3 * rows + TAIL, HD)
    inputs = (queries, keys, values, q_gain.reshape(1, -1), k_gain.reshape(1, -1))
    five = pl.pallas_call(
        shared_rows_kernel,
        grid=(rows // step,),
        in_specs=[whole, whole, whole, gain, gain, SMEM, SMEM],
        out_specs=pl.BlockSpec(shared, lambda i: (0, 0, 0)),
        out_shape=jax.ShapeDtypeStruct(shared, BF16),
        compiler_params=pltpu.CompilerParams(vmem_limit_bytes=VMEM),
        name="shared_rows",
    )(*inputs, block_ids, counts)
    q_rows, kv_rows = pl.pallas_call(
        own_rows_kernel,
        grid=(rows // step,),
        in_specs=[whole, whole, whole, gain, gain],
        out_specs=[
            pl.BlockSpec((heads, step, HD), lambda i: (0, i, 0)),
            pl.BlockSpec((heads, 2, step, HD), lambda i: (0, 0, i, 0)),
        ],
        out_shape=[
            jax.ShapeDtypeStruct((heads, rows, HD), BF16),
            jax.ShapeDtypeStruct((heads, 2, rows, HD), BF16),
        ],
        compiler_params=pltpu.CompilerParams(vmem_limit_bytes=VMEM),
        name="own_rows",
    )(*inputs)
    return five, q_rows, kv_rows


def join_kernel(main_ref, five_ref, out_ref):
    for plane in range(PLANES):
        for lane in range(PER):
            at = (plane * PER + lane) * HD
            if lane < SHARE:
                out_ref[:, at : at + HD] = main_ref[plane * SHARE + lane]
            else:
                out_ref[:, at : at + HD] = five_ref[plane]


def join(main, five):
    rows = main.shape[1]
    step = 32
    width = PLANES * PER * HD
    return pl.pallas_call(
        join_kernel,
        grid=(rows // step,),
        in_specs=[
            pl.BlockSpec((main.shape[0], step, HD), lambda i: (0, i, 0)),
            pl.BlockSpec((PLANES, step, HD), lambda i: (0, i, 0)),
        ],
        out_specs=pl.BlockSpec((step, width), lambda i: (i, 0)),
        out_shape=jax.ShapeDtypeStruct((rows, width), BF16),
        compiler_params=pltpu.CompilerParams(vmem_limit_bytes=HALF),
        name="join_heads",
    )(main, five)


def attend_items(queries, picks, counts, kv, put):
    factor = math.log2(math.e) / math.sqrt(HD)
    ones = jnp.ones((LISTED * BLOCK, HD), BF16)
    scores, tops = [], []
    for query, pick, count in zip(queries, picks, counts):
        keys = jnp.concatenate([kv[p, 0:BLOCK, :] for p in pick], axis=0)
        raw = lax.dot_general(query(), keys, (((1,), (1,)), ((), ())), preferred_element_type=F32)
        parts = []
        for s in range(LISTED):
            bias = jnp.where(s < count, 0.0, -1e30).astype(F32)
            parts.append(raw[:, s * BLOCK : (s + 1) * BLOCK] * factor + bias)
        scores.append(parts)
        tops.append(jnp.max(functools.reduce(jnp.maximum, parts), axis=-1, keepdims=True))
    for i, pick in enumerate(picks):
        weights = jnp.concatenate([jnp.exp2(part - tops[i]).astype(BF16) for part in scores[i]], axis=1)
        values = jnp.concatenate([kv[p, BLOCK : 2 * BLOCK, :] for p in pick], axis=0)
        mixed = jnp.dot(weights, jnp.concatenate([values, ones], axis=1), preferred_element_type=F32)
        put(i, (mixed[:, :HD] / mixed[:, HD:]).astype(BF16))


def fetch(pairs, sems):
    copies = [pltpu.make_async_copy(src, dst, sems.at[i]) for i, (src, dst) in enumerate(pairs)]
    for copy in copies:
        copy.start()
    for copy in copies:
        copy.wait()


def main_kernel(pos_ref, lists_ref, q_ref, all_ref, own_ref, other_ref, out_ref, kv, sems):
    view, c = pl.program_id(0), pos_ref[2]

    @pl.when(view == 0)
    def _():
        pairs = [(all_ref, kv.at[pl.ds(0, 32)])]
        for a in range(2):
            pairs.append((own_ref.at[a], kv.at[pl.ds(32 + 8 * a + 4 * c, 4)]))
            pairs.append((other_ref.at[a], kv.at[pl.ds(32 + 8 * a + 4 * (1 - c), 4)]))
        fetch(pairs, sems)

    queries, picks, counts = [], [], []
    for b in range(8):
        queries.append(functools.partial(lambda b: q_ref[b], b))
        ids = [lists_ref[view, b, s] for s in range(LISTED)]
        picks.append([jnp.where(j < 8, view * 8 + j, 24 + j) for j in ids])
        counts.append(lists_ref[view, b, LISTED])

    def put(i, block):
        out_ref[i] = block

    attend_items(queries, picks, counts, kv, put)


def attend_main(pos, lists, q_all, kv_all, own, other):
    blocks = pl.BlockSpec((8, BLOCK, HD), lambda v: (v, 0, 0))
    return pl.pallas_call(
        main_kernel,
        grid=(4,),
        in_specs=[SMEM, SMEM, blocks, ANY, ANY, ANY],
        out_specs=blocks,
        out_shape=jax.ShapeDtypeStruct(q_all.shape, BF16),
        scratch_shapes=[pltpu.VMEM((SLOTS, 2 * BLOCK, HD), BF16), pltpu.SemaphoreType.DMA((5,))],
        compiler_params=pltpu.CompilerParams(vmem_limit_bytes=HALF),
        cost_estimate=pl.CostEstimate(
            flops=32 * 4 * BLOCK * LISTED * BLOCK * HD,
            bytes_accessed=4 * SLOTS * BLOCK * HD,
            transcendentals=32 * BLOCK * LISTED * BLOCK,
        ),
        name="attend_main",
    )(pos, lists, q_all, kv_all, own, other)


def shared_kernel(pos_ref, lists_ref, five_ref, *rest):
    got, near_ref, far_ref = rest[:3], rest[3], rest[4]
    outs, q, kv, sems = rest[5:9], rest[9], rest[10], rest[11]
    c, y = pos_ref[2], pos_ref[3]
    pairs = [(near_ref, kv.at[pl.ds(8, 8)]), (far_ref, kv.at[pl.ds(16, 8)])]
    for d in range(4):
        mine = five_ref.at[pl.ds(2 * y, 2)] if d == 0 else got[d - 1]
        pairs.append((mine.at[:, pl.ds(0, BLOCK)], q.at[pl.ds(2 * d, 2)]))
        pairs.append((mine.at[:, pl.ds(BLOCK, 2 * BLOCK)], kv.at[pl.ds(2 * d, 2)]))
    fetch(pairs, sems)

    queries, picks, counts = [], [], []
    for i in range(8):
        row = 4 * (i % 2) + lax.rem(y + i // 2, 4)
        queries.append(functools.partial(lambda i: q[i], i))
        pick = []
        for s in range(LISTED):
            j = lists_ref[y, row, s]
            away = lax.rem(lax.rem(j, 4) - y + 4, 4)
            upper = lax.rem(j, 8) // 4
            far = 8 + 8 * lax.rem(upper + c, 2) + 2 * away + j // 8 - 1
            pick.append(jnp.where(j < 8, 2 * away + upper, far))
        picks.append(pick)
        counts.append(lists_ref[y, row, LISTED])

    def put(i, block):
        outs[i // 2][i % 2] = block

    attend_items(queries, picks, counts, kv, put)


def attend_shared(pos, lists, five, got, near, far):
    blocks = pl.BlockSpec((2, BLOCK, HD), lambda i: (0, 0, 0))
    return pl.pallas_call(
        shared_kernel,
        grid=(1,),
        in_specs=[SMEM, SMEM] + [ANY] * 6,
        out_specs=[blocks] * SHARE,
        out_shape=[jax.ShapeDtypeStruct((2, BLOCK, HD), BF16)] * SHARE,
        scratch_shapes=[
            pltpu.VMEM((8, BLOCK, HD), BF16),
            pltpu.VMEM((24, 2 * BLOCK, HD), BF16),
            pltpu.SemaphoreType.DMA((10,)),
        ],
        compiler_params=pltpu.CompilerParams(vmem_limit_bytes=HALF),
        cost_estimate=pl.CostEstimate(
            flops=8 * 4 * BLOCK * LISTED * BLOCK * HD,
            bytes_accessed=4 * 24 * BLOCK * HD,
            transcendentals=8 * BLOCK * LISTED * BLOCK,
        ),
        name="attend_shared",
    )(pos, lists, five, *got, near, far)


def shifted(x, axis, size, by):
    return lax.ppermute(x, axis, [((i + by) % size, i) for i in range(size)])


def ring_kernel(me_ref, *rest):
    parts, out_ref = rest[:-1], rest[-1]
    for r, part in enumerate(parts):
        out_ref[lax.rem(me_ref[0] - r + len(parts), len(parts))] = part[...]


def ordered(me, parts, name):
    count, shape = len(parts), parts[0].shape
    zeros = (0,) * len(shape)
    return pl.pallas_call(
        ring_kernel,
        grid=(1,),
        in_specs=[SMEM] + [pl.BlockSpec(shape, lambda i: zeros)] * count,
        out_specs=pl.BlockSpec((count, *shape), lambda i: (0, *zeros)),
        out_shape=jax.ShapeDtypeStruct((count, *shape), BF16),
        compiler_params=pltpu.CompilerParams(vmem_limit_bytes=HALF),
        name=name,
    )(me.reshape(1), *parts)


def core_half(by_zl, at_zl, at_c):
    c = lax.axis_index("c")
    mine = jnp.stack([lax.dynamic_index_in_dim(by_zl, at_zl[a], 0, keepdims=False) for a in range(2)], axis=1)
    kept = lax.dynamic_index_in_dim(mine, c, 0, keepdims=False)
    sent = lax.dynamic_index_in_dim(mine, 1 - c, 0, keepdims=False)
    here = (at_c == c).reshape((2,) + (1,) * (kept.ndim - 1))
    return jnp.where(here, kept, shifted(sent, "c", 2, 1))


def along_x(half):
    return [half] + [shifted(half, "x", 4, by) for by in (1, 2, 3)]


def true_half(others, at_x):
    away = ((at_x - lax.axis_index("x")) % 4).reshape((2,) + (1,) * (others[0].ndim - 1))
    return jnp.where(
        away < 2,
        jnp.where(away == 0, others[0], others[1]),
        jnp.where(away == 2, others[2], others[3]),
    )


def shards(queries, keys, values, q_gain, k_gain, block_ids, counts, anchors):
    at_zl, at_x, at_c = anchors // 8, (anchors // 2) % 4, anchors % 2
    pos = jnp.stack([lax.axis_index(axis) for axis in ("zl", "zh", "c", "y")])

    five, q_rows, kv_rows = placed(queries, keys, values, q_gain, k_gain, block_ids, counts)
    five = lax.all_to_all(five, PLANE, 0, 0, tiled=True)
    five, kv_rows, q_rows = lax.optimization_barrier((five, kv_rows, q_rows))
    kv_all = lax.all_to_all(kv_rows, EVERY, 0, 0, tiled=True).reshape(32, 2 * BLOCK, HD)

    y = lax.axis_index("y")
    by_view = five.reshape(4, 2, -1, HD)
    lists = by_view[:, 0, 3 * BLOCK : 3 * BLOCK + 8, : LISTED + 1].astype(jnp.int32)
    half = core_half(by_view[:, :, BLOCK : 3 * BLOCK], at_zl, at_c)
    half = true_half(along_x(half), at_x)
    got = []
    for by in (1, 2, 3):
        view = lax.dynamic_index_in_dim(by_view[:, :, : 3 * BLOCK], (y - by) % 4, 0, keepdims=False)
        got.append(shifted(view, "y", 4, by))
    half, *got = lax.optimization_barrier((half, *got))
    near = jnp.concatenate([half] + [shifted(half, "y", 4, by) for by in (1, 2, 3)], axis=0)
    far = shifted(near, "c", 2, 1)
    kv_all, q_rows, near, far, *got = lax.optimization_barrier((kv_all, q_rows, near, far, *got))

    half = core_half(kv_all.reshape(4, 2, 4, 2 * BLOCK, HD), at_zl, at_c)
    half, near, q_rows = lax.optimization_barrier((half, near, q_rows))
    q_all = lax.all_to_all(q_rows, EVERY, 0, 0, tiled=True)
    others = along_x(half)
    parts = attend_shared(pos, lists, five, got, near, far)
    shared = [parts[0]] + [shifted(parts[d], "y", 4, -d) for d in (1, 2, 3)]
    shared = ordered(y, shared, "order_views").reshape(PLANES, BLOCK, HD)
    shared, *others = lax.optimization_barrier((shared, *others))
    shared, q_all = lax.optimization_barrier((shared, q_all))
    home = lax.all_to_all(shared, PLANE, 0, 0, tiled=True)
    own = true_half(others, at_x)
    other = shifted(own, "c", 2, 1)
    mixed = attend_main(pos, lists, q_all, kv_all, own, other)
    main = lax.all_to_all(mixed, EVERY, 0, 0, tiled=True)
    return join(main, home)


def solution(mesh):
    fine = Mesh(mesh.devices.reshape(4, 4, 2, 2, 4), AXES)
    tokens = P(AXES, None)
    frame = ("zl", "x", "c")
    placed = (tokens, tokens, tokens, P(), P(), P(frame, None, None), P(frame, None), P())
    return jax.shard_map(shards, mesh=fine, in_specs=placed, out_specs=tokens, check_vma=False)
```
